128 devices in a mesh: node: 4 (over x), expert: 32 (over z, y, core).
Axes of the slice: x: 4, y: 4, z: 4, core: 2. Of those that a mesh axis runs over, the one named last changes fastest.
Arguments:
- grad_out: bfloat16 [4096, 7168], P(('node', 'expert')), may hold values from -6 to 6
- logits: float32 [4096, 128], P(('node', 'expert')), may hold values from -6 to 6
- routes: int32 [4096, 8], P(('node', 'expert')), may hold values from 0 to 127, as said below
- w_down: bfloat16 [128, 1024, 7168], P(('node', 'expert')), may hold values from -0.1875 to 0.1875
- saved_hidden: bfloat16 [128, 512, 1024], P(('node', 'expert')), may hold values from -4 to 4
Outputs:
- d_hidden: bfloat16 [128, 512, 1024], P(('node', 'expert'))
- d_logits: float32 [4096, 128], P(('node', 'expert'))
The draws below stay inside these ranges and needn't reach their ends.
Inputs may be any that keep to these rules, and one draw needn't show every extreme that they name: `routes`: each row names 8 different experts, four in each of two node groups (expert e lies in group e // 32); one group, drawn from the seed, is named by every row. Among the 32 rows of one device no expert is named by more than 4 rows, and each expert of that group by exactly 4.
All inputs are finite; a program needn't handle non-finite values.
Results may differ from the reference program's by a relative error of at most 0.0049.
Values may be sent and summed in bfloat16 or wider, within the bound.
No kernel may reach another device: no remote copies, remote signals or barrier semaphores. Data moves between devices by JAX's collectives and lax.ppermute only.
A program may use at most 128 MiB of HBM per device.

```python
import jax
import jax.numpy as jnp
from jax import lax

D = 7168
FF = 1024
TOK_DEV = 32
TOKENS = 4096
EXPERTS = 128
MOST = 4
CAP = 512


def draw_routes(key, part):
    key = jax.random.fold_in(key, 11)
    device_count = TOKENS // TOK_DEV
    per_group = EXPERTS // 4
    keys = jax.random.split(key, 6)
    hot_group = jax.random.randint(keys[0], (), 0, 4)
    others = jax.vmap(lambda item: jax.random.permutation(item, 3))(jax.random.split(keys[1], device_count))
    placing = jax.vmap(lambda item: jax.random.permutation(item, TOK_DEV))(jax.random.split(keys[2], device_count))
    hot_index = jax.vmap(lambda item: jax.random.permutation(item, TOK_DEV))(jax.random.split(keys[3], device_count))
    sigma = jax.vmap(lambda item: jax.random.permutation(item, per_group))(jax.random.split(keys[4], device_count * 4))
    sigma = sigma.reshape(device_count, 4, per_group)
    spot = jnp.arange(TOK_DEV, dtype=jnp.int32)
    half_count = TOK_DEV // 2
    quarter_count = TOK_DEV // 4
    which = jnp.where(spot < half_count, 0, jnp.where(spot < half_count + quarter_count, 1, 2))
    start = jnp.where(spot < half_count, 0, jnp.where(spot < half_count + quarter_count, half_count, half_count + quarter_count))
    second_index = spot - start
    second_group = (hot_group + 1 + others[:, which]) % 4
    lanes = jnp.arange(4, dtype=jnp.int32)
    dev_ids = jnp.arange(device_count, dtype=jnp.int32)[:, None, None]
    hot_local = (4 * hot_index[:, :, None] + lanes) % per_group
    second_local = jnp.broadcast_to((4 * second_index[None, :, None] + lanes) % per_group, (device_count, TOK_DEV, 4))
    hot_expert = hot_group * per_group + sigma[dev_ids, hot_group, hot_local]
    second_expand = jnp.broadcast_to(second_group[:, :, None], (device_count, TOK_DEV, 4))
    second_expert = second_expand * per_group + sigma[dev_ids, second_expand, second_local]
    by_position = jnp.concatenate([hot_expert, second_expert], 2).astype(jnp.int32)
    scores = jax.random.randint(keys[5], (device_count, TOK_DEV, 8), 0, 1 << 20) * 8 + jnp.arange(8, dtype=jnp.int32)
    column_order = jnp.argsort(scores, axis=2)
    by_position = jnp.take_along_axis(by_position, column_order, 2)
    rows = jnp.zeros((device_count, TOK_DEV, 8), jnp.int32).at[jnp.arange(device_count)[:, None], placing].set(by_position)
    return rows.reshape(TOKENS, 8)


def block_levels(key, dims, cuts, low, top_value):
    gain, own = 1.0, jax.random.fold_in(key, 6)
    for dim, blocks in cuts:
        draws = jnp.exp(jax.random.uniform(jax.random.fold_in(own, dim), (blocks,), jnp.float32, low / len(cuts), top_value / len(cuts)))
        gain = gain * jnp.repeat(draws, dims[dim] // blocks).reshape([-1 if axis == dim else 1 for axis in range(len(dims))])
    return gain


def normal_values(stream_key, dims, scale, limit, cuts=(), kind=jnp.bfloat16):
    array = scale * jax.random.normal(stream_key, dims, jnp.float32)
    if cuts:
        array = array * block_levels(stream_key, dims, cuts, -0.22, 0.18)
    return jnp.clip(array, -limit, limit).astype(kind)


def setup_inputs(seed: int = 0) -> dict:
    key_list = jax.random.split(jax.random.key(seed), 6)
    return {
        "grad_out": normal_values(key_list[0], (TOKENS, D), 1.0, 6.0, ((0, 128),)),
        "logits": normal_values(key_list[1], (TOKENS, EXPERTS), 1.5, 6.0, ((0, 128),), jnp.float32),
        "routes": draw_routes(jax.random.fold_in(key_list[5], 71), 0),
        "w_down": normal_values(key_list[3], (EXPERTS, FF, D), FF ** -0.5, 0.1875, ((0, 128),)),
        "saved_hidden": normal_values(key_list[4], (EXPERTS, CAP, FF), 0.25, 4.0, ((0, 128),)),
    }


route_scale = 2.5


def reference(grad_out, logits, routes, w_down, saved_hidden):
    device_count = TOKENS // TOK_DEV
    expert_ids = jnp.arange(EXPERTS, dtype=jnp.int32)
    picked = (routes[:, :, None] == expert_ids).astype(jnp.int32)
    routed = jnp.sum(picked, 1)
    blocks = routed.reshape(device_count, TOK_DEV, EXPERTS)
    earlier = (jnp.cumsum(blocks, 1) - blocks).reshape(TOKENS, EXPERTS)
    position = jnp.take_along_axis(earlier, routes, 1)
    source = (jnp.arange(TOKENS, dtype=jnp.int32) // TOK_DEV)[:, None]
    slot_index = (source * MOST + position).astype(jnp.int32)
    affinity = jax.nn.sigmoid(logits)
    chosen = jnp.take_along_axis(affinity, routes, 1)
    total = jnp.sum(chosen, 1, keepdims=True)
    weights = (route_scale * chosen / total).astype(jnp.bfloat16)
    token_ids = jnp.broadcast_to(jnp.arange(TOKENS, dtype=jnp.int32)[:, None], routes.shape)
    token_of = jnp.full((EXPERTS, CAP), -1, jnp.int32).at[routes, slot_index].set(token_ids)
    weight_of = jnp.zeros((EXPERTS, CAP), jnp.bfloat16).at[routes, slot_index].set(weights)

    def one_expert(operands):
        table, slot_weight, weight, hidden = operands
        live = table >= 0
        rows = jnp.where(live[:, None], grad_out[jnp.maximum(table, 0)], jnp.zeros((), jnp.bfloat16))
        raw = jnp.dot(rows, weight.T, preferred_element_type=jnp.float32)
        grad_hidden = (slot_weight.astype(jnp.float32)[:, None] * raw).astype(jnp.bfloat16)
        route_grad = jnp.sum(raw * hidden.astype(jnp.float32), 1)
        return grad_hidden, route_grad

    d_hidden, route_grad = lax.map(one_expert, (token_of, weight_of, w_down, saved_hidden))
    per_route = route_grad[routes, slot_index]
    mean_grad = jnp.sum(per_route * chosen, 1, keepdims=True) / total
    d_chosen = (route_scale / total) * (per_route - mean_grad)
    d_affinity = d_chosen * chosen * (1.0 - chosen)
    d_logits = jnp.sum(picked.astype(jnp.float32) * d_affinity[:, :, None], 1)
    return d_hidden, d_logits
```

```python
import functools

import jax
import jax.numpy as jnp
from jax import lax
from jax.experimental import pallas as pl
from jax.experimental.pallas import tpu as pltpu
from jax.sharding import PartitionSpec as P

route_scale = 2.5
QUARTERS = 4
PIECE = 256
MIB = 1 << 20


def iota(shape, dim):
    return lax.broadcasted_iota(jnp.int32, shape, dim)


def slot_ranks(routes_t, experts):
    most, tokens = routes_t.shape
    ids = iota((experts, tokens), 0)
    picked = jnp.zeros((experts, tokens), jnp.float32)
    for k in range(most):
        picked += (routes_t[k : k + 1, :] == ids).astype(jnp.float32)
    before = (iota((tokens, tokens), 0) < iota((tokens, tokens), 1)).astype(jnp.bfloat16)
    earlier = jnp.dot(picked.astype(jnp.bfloat16), before, preferred_element_type=jnp.float32)
    return picked * (earlier + 1.0)


def pack_kernel(slots, routes_ref, grad_ref, out_ref, ranks, pieces):
    tokens, width = grad_ref.shape
    experts = ranks.shape[0]
    span = QUARTERS * PIECE

    @pl.when(pl.program_id(0) == 0)
    def _():
        found = slot_ranks(routes_ref[...], experts).astype(jnp.bfloat16)
        ranks[...] = jnp.concatenate([found] * QUARTERS, 1)
        for step in range(width // span):
            for q in range(QUARTERS):
                pieces[q * tokens : (q + 1) * tokens, step * PIECE : (step + 1) * PIECE] = grad_ref[
                    :, step * span + q * PIECE : step * span + (q + 1) * PIECE
                ]

    rows, columns = out_ref.shape[0], QUARTERS * tokens
    unit = QUARTERS * slots
    row = iota((rows, experts), 0) + pl.program_id(0) * rows
    spread = (row // unit == iota((rows, experts), 1)).astype(jnp.bfloat16)
    rank = jnp.dot(spread, ranks[...], preferred_element_type=jnp.float32)
    row = iota((rows, columns), 0)
    slot = (row % slots + 1).astype(jnp.float32)
    same = (row // slots) % QUARTERS == iota((rows, columns), 1) // tokens
    take = jnp.where(same & (rank == slot), 1.0, 0.0).astype(jnp.bfloat16)
    out_ref[...] = jnp.dot(take, pieces[...], preferred_element_type=jnp.float32).astype(jnp.bfloat16)


def weight_kernel(slots, routes_ref, logits_ref, out_ref, rank_ref, chosen_ref):
    tokens, experts = logits_ref.shape
    found = slot_ranks(routes_ref[...], experts).astype(jnp.bfloat16)
    unit = (iota((experts, experts), 0) == iota((experts, experts), 1)).astype(jnp.bfloat16)
    rank = lax.dot_general(found, unit, (((0,), (0,)), ((), ())), preferred_element_type=jnp.float32)
    rank_ref[...] = rank
    chosen = jnp.where(rank > 0.0, jax.nn.sigmoid(logits_ref[...]), 0.0)
    chosen_ref[...] = chosen
    total = jnp.sum(chosen, 1, keepdims=True)
    weights = (route_scale * chosen / total).astype(jnp.bfloat16).astype(jnp.float32)
    out = jnp.zeros((experts, experts), jnp.float32)
    lane = iota((tokens, experts), 1)
    for j in range(slots):
        mine = jnp.where(rank == j + 1.0, weights, 0.0).astype(jnp.bfloat16)
        to = (lane == slots + j).astype(jnp.bfloat16)
        out += lax.dot_general(mine, to, (((0,), (0,)), ((), ())), preferred_element_type=jnp.float32)
    out_ref[...] = out


def expert_kernel(slots, rows_ref, w_ref, hidden_ref, weights_ref, raw_ref, back_ref, rows):
    unit = QUARTERS * slots
    step = pl.program_id(0)
    block = 256
    each = block // QUARTERS
    to, came = iota((block, block), 0), iota((block, block), 1)
    source = (to % each) // slots * unit + to // each * slots + to % slots
    order = (came == source).astype(jnp.bfloat16)
    for b in range(rows_ref.shape[0] // block):
        turned = jnp.dot(
            order, rows_ref[b * block : (b + 1) * block, :], preferred_element_type=jnp.float32
        ).astype(jnp.bfloat16)
        for q in range(QUARTERS):
            rows[b * each : (b + 1) * each, q * PIECE : (q + 1) * PIECE] = turned[q * each : (q + 1) * each]
    part = lax.dot_general(
        rows[...], w_ref[...], (((1,), (1,)), ((), ())), preferred_element_type=jnp.float32
    )

    @pl.when(step == 0)
    def _():
        raw_ref[...] = part

    @pl.when(step > 0)
    def _():
        raw_ref[...] += part

    @pl.when(step == pl.num_programs(0) - 1)
    def _():
        capacity = raw_ref.shape[0]
        peers, lanes = back_ref.shape
        grads = jnp.sum(raw_ref[...] * hidden_ref[...].astype(jnp.float32), 1, keepdims=True)
        slot = iota((capacity, lanes), 0) % slots
        spread = jnp.where(slot == iota((capacity, lanes), 1), grads, 0.0)
        gather = (iota((peers, capacity), 0) == iota((peers, capacity), 1) // slots).astype(jnp.float32)
        back_ref[...] = weights_ref[...] + jnp.dot(
            gather, spread, preferred_element_type=jnp.float32, precision=lax.Precision.HIGHEST
        )


def final_kernel(slots, raw_ref, back_ref, rank_ref, chosen_ref, hidden_ref, logits_ref):
    block = raw_ref.shape[0]
    peers = block // slots
    lanes = back_ref.shape[1]
    start = pl.multiple_of(pl.program_id(0) * peers, peers)
    mine = back_ref[pl.ds(start, peers), :].astype(jnp.bfloat16)
    spread = (iota((block, peers), 0) // slots == iota((block, peers), 1)).astype(jnp.bfloat16)
    weight = jnp.dot(spread, mine, preferred_element_type=jnp.float32)
    slot = iota((block, lanes), 0) % slots
    weight = jnp.sum(jnp.where(slot + slots == iota((block, lanes), 1), weight, 0.0), 1, keepdims=True)
    hidden_ref[...] = (weight * raw_ref[...]).astype(jnp.bfloat16)

    @pl.when(pl.program_id(0) == 0)
    def _():
        rank = rank_ref[...]
        chosen = chosen_ref[...]
        total = jnp.sum(chosen, 1, keepdims=True)
        back = jnp.transpose(back_ref[...])
        per_route = jnp.zeros_like(chosen)
        for j in range(slots):
            per_route += jnp.where(rank == j + 1.0, back[j : j + 1, :], 0.0)
        mean_grad = jnp.sum(per_route * chosen, 1, keepdims=True) / total
        d_chosen = (route_scale / total) * (per_route - mean_grad)
        logits_ref[...] = jnp.where(rank > 0.0, d_chosen * chosen * (1.0 - chosen), 0.0)


def whole(shape):
    return pl.BlockSpec(shape, lambda i: (0,) * len(shape))


def params():
    return pltpu.CompilerParams(vmem_limit_bytes=40 * MIB)


def shards(grad_out, logits, routes, w_down, saved_hidden):
    tokens, width = grad_out.shape
    experts = logits.shape[1]
    capacity, units = saved_hidden.shape[1:]
    slots = capacity // experts
    unit = QUARTERS * slots
    narrow = width // QUARTERS
    routes_t = routes.T
    pack_rows = 256
    sent = pl.pallas_call(
        functools.partial(pack_kernel, slots),
        grid=(experts * unit // pack_rows,),
        in_specs=[whole(routes_t.shape), whole(grad_out.shape)],
        out_specs=pl.BlockSpec((pack_rows, narrow), lambda i: (i, 0)),
        out_shape=jax.ShapeDtypeStruct((experts * unit, narrow), jnp.bfloat16),
        scratch_shapes=[
            pltpu.VMEM((experts, QUARTERS * tokens), jnp.bfloat16),
            pltpu.VMEM((QUARTERS * tokens, narrow), jnp.bfloat16),
        ],
        compiler_params=params(),
        cost_estimate=pl.CostEstimate(
            flops=2 * experts * unit * narrow * QUARTERS * tokens,
            bytes_accessed=2 * experts * unit * narrow,
            transcendentals=0,
        ),
        name="pack",
    )(routes_t, grad_out)
    arrived = lax.all_to_all(
        sent.reshape(experts, unit, narrow), ("node", "expert"), split_axis=0, concat_axis=0, tiled=True
    ).reshape(experts * unit, narrow)
    weights, rank, chosen = pl.pallas_call(
        functools.partial(weight_kernel, slots),
        out_shape=(
            jax.ShapeDtypeStruct((experts, experts), jnp.float32),
            jax.ShapeDtypeStruct((tokens, experts), jnp.float32),
            jax.ShapeDtypeStruct((tokens, experts), jnp.float32),
        ),
        compiler_params=params(),
        name="weights",
    )(routes_t, logits)
    span = QUARTERS * PIECE
    raw, back = pl.pallas_call(
        functools.partial(expert_kernel, slots),
        grid=(width // span,),
        in_specs=[
            pl.BlockSpec((experts * unit, PIECE), lambda i: (0, i)),
            pl.BlockSpec((None, units, span), lambda i: (0, 0, i)),
            pl.BlockSpec((None, capacity, units), lambda i: (0, 0, 0)),
            whole((experts, experts)),
        ],
        out_specs=(whole((capacity, units)), whole((experts, experts))),
        out_shape=(
            jax.ShapeDtypeStruct((capacity, units), jnp.float32),
            jax.ShapeDtypeStruct((experts, experts), jnp.float32),
        ),
        scratch_shapes=[pltpu.VMEM((capacity, span), jnp.bfloat16)],
        compiler_params=params(),
        cost_estimate=pl.CostEstimate(
            flops=2 * capacity * units * width,
            bytes_accessed=2 * (units + capacity) * width + 4 * capacity * units,
            transcendentals=0,
        ),
        name="expert",
    )(arrived, w_down, saved_hidden, weights)
    returned = lax.all_to_all(
        back.reshape(experts, 1, experts), ("node", "expert"), split_axis=0, concat_axis=0, tiled=True
    ).reshape(experts, experts)
    final_rows = capacity // 4
    d_hidden, d_logits = pl.pallas_call(
        functools.partial(final_kernel, slots),
        grid=(4,),
        in_specs=[
            pl.BlockSpec((final_rows, units), lambda i: (i, 0)),
            whole((experts, experts)),
            whole((tokens, experts)),
            whole((tokens, experts)),
        ],
        out_specs=(
            pl.BlockSpec((None, final_rows, units), lambda i: (0, i, 0)),
            whole((tokens, experts)),
        ),
        out_shape=(
            jax.ShapeDtypeStruct((1, capacity, units), jnp.bfloat16),
            jax.ShapeDtypeStruct((tokens, experts), jnp.float32),
        ),
        compiler_params=params(),
        name="final",
    )(raw, returned, rank, chosen)
    return (d_hidden, d_logits)


def solution(mesh):
    return jax.shard_map(
        shards,
        mesh=mesh,
        in_specs=(
            P(("node", "expert"), None),
            P(("node", "expert"), None),
            P(("node", "expert"), None),
            P(("node", "expert"), None, None),
            P(("node", "expert"), None, None),
        ),
        out_specs=(P(("node", "expert"), None, None), P(("node", "expert"), None)),
        check_vma=False,
    )
```

```python
import functools

import jax
import jax.numpy as jnp
from jax import lax
from jax.experimental import pallas as pl
from jax.experimental.pallas import tpu as pltpu
from jax.sharding import PartitionSpec as P

route_scale = 2.5
QUARTERS = 4
PIECE = 256
MIB = 1 << 20


def iota(shape, dim):
    return lax.broadcasted_iota(jnp.int32, shape, dim)


def slot_ranks(routes_t, experts):
    most, tokens = routes_t.shape
    ids = iota((experts, tokens), 0)
    picked = jnp.zeros((experts, tokens), jnp.float32)
    for k in range(most):
        picked += (routes_t[k : k + 1, :] == ids).astype(jnp.float32)
    before = (iota((tokens, tokens), 0) < iota((tokens, tokens), 1)).astype(jnp.bfloat16)
    earlier = jnp.dot(picked.astype(jnp.bfloat16), before, preferred_element_type=jnp.float32)
    return picked * (earlier + 1.0)


def pack_kernel(slots, routes_ref, grad_ref, out_hbm, ranks, pieces, out, sems):
    tokens, width = grad_ref.shape
    experts = ranks.shape[0]
    span = QUARTERS * PIECE
    found = slot_ranks(routes_ref[...], experts).astype(jnp.bfloat16)
    ranks[...] = jnp.concatenate([found] * QUARTERS, 1)
    for step in range(width // span):
        for q in range(QUARTERS):
            pieces[q * tokens : (q + 1) * tokens, step * PIECE : (step + 1) * PIECE] = grad_ref[
                :, step * span + q * PIECE : step * span + (q + 1) * PIECE
            ]
    blocks = sems.shape[0]
    rows, columns = out.shape[0] // blocks, QUARTERS * tokens
    unit = QUARTERS * slots

    def copy(b):
        at = pl.ds(pl.multiple_of(b * rows, rows), rows)
        return pltpu.make_async_copy(out.at[at, :], out_hbm.at[at, :], sems.at[b])

    @pl.loop(0, blocks)
    def _(b):
        row = iota((rows, experts), 0) + b * rows
        spread = (row // unit == iota((rows, experts), 1)).astype(jnp.bfloat16)
        rank = jnp.dot(spread, ranks[...], preferred_element_type=jnp.float32)
        row = iota((rows, columns), 0)
        slot = (row % slots + 1).astype(jnp.float32)
        same = (row // slots) % QUARTERS == iota((rows, columns), 1) // tokens
        take = jnp.where(same & (rank == slot), 1.0, 0.0).astype(jnp.bfloat16)
        at = pl.ds(pl.multiple_of(b * rows, rows), rows)
        out[at, :] = jnp.dot(take, pieces[...], preferred_element_type=jnp.float32).astype(jnp.bfloat16)
        copy(b).start()

    @pl.loop(0, blocks)
    def _(b):
        copy(b).wait()


def weight_kernel(slots, routes_ref, logits_ref, out_ref, rank_ref, chosen_ref):
    tokens, experts = logits_ref.shape
    found = slot_ranks(routes_ref[...], experts).astype(jnp.bfloat16)
    unit = (iota((experts, experts), 0) == iota((experts, experts), 1)).astype(jnp.bfloat16)
    rank = lax.dot_general(found, unit, (((0,), (0,)), ((), ())), preferred_element_type=jnp.float32)
    rank_ref[...] = rank
    chosen = jnp.where(rank > 0.0, jax.nn.sigmoid(logits_ref[...]), 0.0)
    chosen_ref[...] = chosen
    total = jnp.sum(chosen, 1, keepdims=True)
    weights = (route_scale * chosen / total).astype(jnp.bfloat16).astype(jnp.float32)
    out = jnp.zeros((experts, experts), jnp.float32)
    lane = iota((tokens, experts), 1)
    for j in range(slots):
        mine = jnp.where(rank == j + 1.0, weights, 0.0).astype(jnp.bfloat16)
        to = (lane == slots + j).astype(jnp.bfloat16)
        out += lax.dot_general(mine, to, (((0,), (0,)), ((), ())), preferred_element_type=jnp.float32)
    out_ref[...] = out


def project_kernel(slots, hidden_ref, w_ref, out_ref):
    block = 256
    each = block // QUARTERS
    unit = QUARTERS * slots
    to, came = iota((block, block), 0), iota((block, block), 1)
    source = (to // slots) % QUARTERS * each + to // unit * slots + to % slots
    order = (came == source).astype(jnp.bfloat16)
    whole = jnp.dot(hidden_ref[...], w_ref[...], preferred_element_type=jnp.float32).astype(jnp.bfloat16)
    for b in range(out_ref.shape[0] // block):
        rows = whole[b * each : (b + 1) * each]
        stacked = jnp.concatenate([rows[:, q * PIECE : (q + 1) * PIECE] for q in range(QUARTERS)], 0)
        out_ref[b * block : (b + 1) * block, :] = jnp.dot(
            order, stacked, preferred_element_type=jnp.float32
        ).astype(jnp.bfloat16)


def return_kernel(slots, rows_hbm, project_hbm, weights_ref, back_ref, rows, project, row_sems, project_sems):
    blocks = row_sems.shape[0]
    block, narrow = rows.shape[0] // blocks, rows.shape[1]
    unit = QUARTERS * slots
    lanes = back_ref.shape[1]
    part = 128

    def copies(b):
        at = pl.ds(pl.multiple_of(b * block, block), block)
        return (
            pltpu.make_async_copy(rows_hbm.at[at, :], rows.at[at, :], row_sems.at[b]),
            pltpu.make_async_copy(project_hbm.at[at, :], project.at[at, :], project_sems.at[b]),
        )

    for b in range(blocks):
        for copy in copies(b):
            copy.start()

    @pl.loop(0, blocks)
    def _(b):
        for copy in copies(b):
            copy.wait()
        for start in range(0, block, part):
            at = pl.ds(pl.multiple_of(b * block + start, part), part)
            product = rows[at, :].astype(jnp.float32) * project[at, :].astype(jnp.float32)
            total = product[:, :lanes]
            for column in range(lanes, narrow, lanes):
                total += product[:, column : column + lanes]
            grads = jnp.sum(total, 1, keepdims=True)
            slot = iota((part, lanes), 0) % slots
            spread = jnp.where(slot == iota((part, lanes), 1), grads, 0.0)
            peers = part // unit
            to = pl.ds(pl.multiple_of(b * (block // unit) + start // unit, peers), peers)
            back_ref[to, :] = weights_ref[to, :] + jnp.sum(spread.reshape(peers, unit, lanes), 1)


def expert_kernel(slots, rows_hbm, w_hbm, raw_ref, arrived, rows, w, row_sems, w_sems):
    block = 256
    each = block // QUARTERS
    unit = QUARTERS * slots
    blocks = arrived.shape[0] // block
    tiles = w_sems.shape[0]
    tile = w.shape[0] // tiles

    def row_copy(b):
        at = pl.ds(pl.multiple_of(b * block, block), block)
        return pltpu.make_async_copy(rows_hbm.at[at, :], arrived.at[at, :], row_sems.at[b])

    def w_copy(n):
        at = pl.ds(pl.multiple_of(n * tile, tile), tile)
        return pltpu.make_async_copy(w_hbm.at[0, at, :], w.at[at, :], w_sems.at[n])

    for b in range(blocks):
        row_copy(b).start()
    to, came = iota((block, block), 0), iota((block, block), 1)
    source = (to % each) // slots * unit + to // each * slots + to % slots
    order = (came == source).astype(jnp.bfloat16)

    @pl.loop(0, blocks)
    def _(b):
        row_copy(b).wait()

        @pl.when(b % (blocks // tiles) == blocks // tiles - 1)
        def _():
            w_copy(b // (blocks // tiles)).start()

        at = pl.ds(pl.multiple_of(b * block, block), block)
        to = pl.ds(pl.multiple_of(b * each, each), each)
        for step in range(arrived.shape[1] // PIECE):
            turned = jnp.dot(
                order, arrived[at, step * PIECE : (step + 1) * PIECE], preferred_element_type=jnp.float32
            ).astype(jnp.bfloat16)
            for q in range(QUARTERS):
                column = (step * QUARTERS + q) * PIECE
                rows[to, column : column + PIECE] = turned[q * each : (q + 1) * each]

    @pl.loop(0, tiles)
    def _(n):
        w_copy(n).wait()
        at = pl.ds(pl.multiple_of(n * tile, tile), tile)
        raw_ref[:, at] = lax.dot_general(
            rows[...], w[at, :], (((1,), (1,)), ((), ())), preferred_element_type=jnp.float32
        )


def final_kernel(slots, raw_ref, back_ref, rank_ref, chosen_ref, hidden_ref, logits_ref):
    block = raw_ref.shape[0]
    peers = block // slots
    lanes = back_ref.shape[1]
    start = pl.multiple_of(pl.program_id(0) * peers, peers)
    mine = back_ref[pl.ds(start, peers), :].astype(jnp.bfloat16)
    spread = (iota((block, peers), 0) // slots == iota((block, peers), 1)).astype(jnp.bfloat16)
    weight = jnp.dot(spread, mine, preferred_element_type=jnp.float32)
    slot = iota((block, lanes), 0) % slots
    weight = jnp.sum(jnp.where(slot + slots == iota((block, lanes), 1), weight, 0.0), 1, keepdims=True)
    hidden_ref[...] = (weight * raw_ref[...]).astype(jnp.bfloat16)

    @pl.when(pl.program_id(0) == 0)
    def _():
        rank = rank_ref[...]
        chosen = chosen_ref[...]
        total = jnp.sum(chosen, 1, keepdims=True)
        back = jnp.transpose(back_ref[...])
        per_route = jnp.zeros_like(chosen)
        for j in range(slots):
            per_route += jnp.where(rank == j + 1.0, back[j : j + 1, :], 0.0)
        mean_grad = jnp.sum(per_route * chosen, 1, keepdims=True) / total
        d_chosen = (route_scale / total) * (per_route - mean_grad)
        logits_ref[...] = jnp.where(rank > 0.0, d_chosen * chosen * (1.0 - chosen), 0.0)


def whole(shape):
    return pl.BlockSpec(shape, lambda i: (0,) * len(shape))


def params(size=24):
    return pltpu.CompilerParams(vmem_limit_bytes=size * MIB)


def in_hbm(array):
    return pltpu.with_memory_space_constraint(array, pltpu.HBM)


def shards(grad_out, logits, routes, w_down, saved_hidden):
    tokens, width = grad_out.shape
    experts = logits.shape[1]
    capacity, units = saved_hidden.shape[1:]
    slots = capacity // experts
    unit = QUARTERS * slots
    narrow = width // QUARTERS
    routes_t = routes.T
    near, far = pl.BlockSpec(memory_space=pltpu.VMEM), pl.BlockSpec(memory_space=pltpu.HBM)
    sent = pl.pallas_call(
        functools.partial(pack_kernel, slots),
        in_specs=[near, near],
        out_specs=far,
        out_shape=pltpu.HBM((experts * unit, narrow), jnp.bfloat16),
        scratch_shapes=[
            pltpu.VMEM((experts, QUARTERS * tokens), jnp.bfloat16),
            pltpu.VMEM((QUARTERS * tokens, narrow), jnp.bfloat16),
            pltpu.VMEM((experts * unit, narrow), jnp.bfloat16),
            pltpu.SemaphoreType.DMA((8,)),
        ],
        compiler_params=params(),
        cost_estimate=pl.CostEstimate(
            flops=2 * experts * unit * narrow * QUARTERS * tokens,
            bytes_accessed=2 * experts * unit * narrow,
            transcendentals=0,
        ),
        name="pack",
    )(in_hbm(routes_t), in_hbm(grad_out))
    arrived = lax.all_to_all(
        sent.reshape(experts, unit, narrow), ("node", "expert"), split_axis=0, concat_axis=0, tiled=True
    ).reshape(experts * unit, narrow)
    weights, rank, chosen = pl.pallas_call(
        functools.partial(weight_kernel, slots),
        out_shape=(
            jax.ShapeDtypeStruct((experts, experts), jnp.float32),
            jax.ShapeDtypeStruct((tokens, experts), jnp.float32),
            jax.ShapeDtypeStruct((tokens, experts), jnp.float32),
        ),
        compiler_params=params(),
        name="weights",
    )(routes_t, logits)
    span = QUARTERS * PIECE
    project = pl.pallas_call(
        functools.partial(project_kernel, slots),
        grid=(width // span,),
        in_specs=[
            pl.BlockSpec((None, capacity, units), lambda i: (0, 0, 0)),
            pl.BlockSpec((None, units, span), lambda i: (0, 0, i)),
        ],
        out_specs=pl.BlockSpec((experts * unit, PIECE), lambda i: (0, i)),
        out_shape=pltpu.HBM((experts * unit, narrow), jnp.bfloat16),
        compiler_params=params(),
        cost_estimate=pl.CostEstimate(
            flops=2 * capacity * units * width, bytes_accessed=2 * units * width, transcendentals=0
        ),
        name="project",
    )(saved_hidden, in_hbm(w_down))
    back = pl.pallas_call(
        functools.partial(return_kernel, slots),
        in_specs=[far, far, near],
        out_specs=near,
        out_shape=jax.ShapeDtypeStruct((experts, experts), jnp.float32),
        scratch_shapes=[
            pltpu.VMEM((experts * unit, narrow), jnp.bfloat16),
            pltpu.VMEM((experts * unit, narrow), jnp.bfloat16),
            pltpu.SemaphoreType.DMA((8,)),
            pltpu.SemaphoreType.DMA((8,)),
        ],
        compiler_params=params(),
        cost_estimate=pl.CostEstimate(
            flops=2 * capacity * width, bytes_accessed=4 * capacity * width, transcendentals=0
        ),
        name="return",
    )(in_hbm(arrived), in_hbm(project), weights)
    raw = pl.pallas_call(
        functools.partial(expert_kernel, slots),
        in_specs=[far, far],
        out_shape=jax.ShapeDtypeStruct((capacity, units), jnp.float32),
        scratch_shapes=[
            pltpu.VMEM((experts * unit, narrow), jnp.bfloat16),
            pltpu.VMEM((capacity, width), jnp.bfloat16),
            pltpu.VMEM((units, width), jnp.bfloat16),
            pltpu.SemaphoreType.DMA((experts * unit // 256,)),
            pltpu.SemaphoreType.DMA((units // 256,)),
        ],
        compiler_params=params(48),
        cost_estimate=pl.CostEstimate(
            flops=2 * capacity * units * width,
            bytes_accessed=2 * (units + capacity) * width + 4 * capacity * units,
            transcendentals=0,
        ),
        name="expert",
    )(in_hbm(arrived), in_hbm(w_down))
    returned = lax.all_to_all(
        back.reshape(experts, 1, experts), ("node", "expert"), split_axis=0, concat_axis=0, tiled=True
    ).reshape(experts, experts)
    final_rows = capacity // 4
    d_hidden, d_logits = pl.pallas_call(
        functools.partial(final_kernel, slots),
        grid=(4,),
        in_specs=[
            pl.BlockSpec((final_rows, units), lambda i: (i, 0)),
            whole((experts, experts)),
            whole((tokens, experts)),
            whole((tokens, experts)),
        ],
        out_specs=(
            pl.BlockSpec((None, final_rows, units), lambda i: (0, i, 0)),
            whole((tokens, experts)),
        ),
        out_shape=(
            jax.ShapeDtypeStruct((1, capacity, units), jnp.bfloat16),
            jax.ShapeDtypeStruct((tokens, experts), jnp.float32),
        ),
        compiler_params=params(),
        name="final",
    )(raw, returned, rank, chosen)
    return (d_hidden, d_logits)


def solution(mesh):
    return jax.shard_map(
        shards,
        mesh=mesh,
        in_specs=(
            P(("node", "expert"), None),
            P(("node", "expert"), None),
            P(("node", "expert"), None),
            P(("node", "expert"), None, None),
            P(("node", "expert"), None, None),
        ),
        out_specs=(P(("node", "expert"), None, None), P(("node", "expert"), None)),
        check_vma=False,
    )
```

```python
import functools

import jax
import jax.numpy as jnp
from jax import lax
from jax.experimental import pallas as pl
from jax.experimental.pallas import tpu as pltpu
from jax.sharding import PartitionSpec as P

route_scale = 2.5
MIB = 1 << 20


def iota(shape, dim):
    return lax.broadcasted_iota(jnp.int32, shape, dim)


def slot_ranks(routes_t, experts):
    most, tokens = routes_t.shape
    ids = iota((experts, tokens), 0)
    picked = jnp.zeros((experts, tokens), jnp.float32)
    for k in range(most):
        picked += (routes_t[k : k + 1, :] == ids).astype(jnp.float32)
    before = (iota((tokens, tokens), 0) < iota((tokens, tokens), 1)).astype(jnp.bfloat16)
    earlier = jnp.dot(picked.astype(jnp.bfloat16), before, preferred_element_type=jnp.float32)
    return picked * (earlier + 1.0)


def pack_kernel(slots, routes_ref, grad_ref, out_hbm, out, sems):
    tokens, width = grad_ref.shape
    experts = out.shape[0]
    rows = experts * slots
    rank = slot_ranks(routes_ref[...], experts)
    rank = jnp.broadcast_to(rank[:, None, :], (experts, slots, tokens)).reshape(rows, tokens)
    slot = (iota((rows, tokens), 0) % slots + 1).astype(jnp.float32)
    take = jnp.where(rank == slot, 1.0, 0.0).astype(jnp.bfloat16)
    parts = sems.shape[0]
    part = width // parts

    def copy(c):
        at = pl.ds(c * part, part)
        return pltpu.make_async_copy(out.at[:, :, at], out_hbm.at[:, :, at], sems.at[c])

    for c in range(parts):
        at = pl.ds(c * part, part)
        packed = jnp.dot(take, grad_ref[:, at], preferred_element_type=jnp.float32).astype(jnp.bfloat16)
        out[:, :, at] = packed.reshape(experts, slots, part)
        copy(c).start()
    for c in range(parts):
        copy(c).wait()


def weight_kernel(slots, routes_ref, logits_ref, out_ref, rank_ref, chosen_ref):
    tokens, experts = logits_ref.shape
    found = slot_ranks(routes_ref[...], experts).astype(jnp.bfloat16)
    unit = (iota((experts, experts), 0) == iota((experts, experts), 1)).astype(jnp.bfloat16)
    rank = lax.dot_general(found, unit, (((0,), (0,)), ((), ())), preferred_element_type=jnp.float32)
    rank_ref[...] = rank
    chosen = jnp.where(rank > 0.0, jax.nn.sigmoid(logits_ref[...]), 0.0)
    chosen_ref[...] = chosen
    total = jnp.sum(chosen, 1, keepdims=True)
    weights = (route_scale * chosen / total).astype(jnp.bfloat16).astype(jnp.float32)
    out = jnp.zeros((experts, experts), jnp.float32)
    lane = iota((tokens, experts), 1)
    for j in range(slots):
        mine = jnp.where(rank == j + 1.0, weights, 0.0).astype(jnp.bfloat16)
        to = (lane == slots + j).astype(jnp.bfloat16)
        out += lax.dot_general(mine, to, (((0,), (0,)), ((), ())), preferred_element_type=jnp.float32)
    out_ref[...] = out


def project_kernel(hidden_ref, w_ref, out_ref):
    out_ref[...] = jnp.dot(hidden_ref[...], w_ref[...], preferred_element_type=jnp.float32).astype(jnp.bfloat16)


def return_kernel(rows_hbm, project_hbm, weights_ref, back_ref, rows, project, row_sems, project_sems):
    blocks = row_sems.shape[0]
    slots, width = rows.shape[1:]
    peers = rows.shape[0] // blocks
    lanes = back_ref.shape[1]
    part, wide = 8, 1024

    def copies(b):
        at = pl.ds(pl.multiple_of(b * peers, peers), peers)
        to = pl.ds(pl.multiple_of(b * peers * slots, peers * slots), peers * slots)
        return (
            pltpu.make_async_copy(rows_hbm.at[at], rows.at[at], row_sems.at[b]),
            pltpu.make_async_copy(project_hbm.at[to, :], project.at[to, :], project_sems.at[b]),
        )

    for b in range(blocks):
        for copy in copies(b):
            copy.start()

    @pl.loop(0, blocks)
    def _(b):
        for copy in copies(b):
            copy.wait()
        for start in range(0, peers, part):
            at = pl.ds(pl.multiple_of(b * peers + start, part), part)
            to = pl.ds(pl.multiple_of((b * peers + start) * slots, part * slots), part * slots)
            total = jnp.zeros((part * slots, lanes), jnp.float32)
            for begin in range(0, width, wide):
                columns = slice(begin, begin + wide)
                row = rows[at, :, columns].reshape(part * slots, wide).astype(jnp.float32)
                product = row * project[to, columns].astype(jnp.float32)
                for column in range(0, wide, lanes):
                    total += product[:, column : column + lanes]
            grads = jnp.sum(total, 1, keepdims=True)
            slot = iota((part * slots, lanes), 0) % slots
            spread = jnp.where(slot == iota((part * slots, lanes), 1), grads, 0.0)
            back_ref[at, :] = weights_ref[at, :] + jnp.sum(spread.reshape(part, slots, lanes), 1)


def expert_kernel(rows_hbm, w_hbm, raw_ref, arrived, rows, w, row_sems, w_sems):
    blocks, tiles = row_sems.shape[0], w_sems.shape[0]
    peers = arrived.shape[0] // blocks
    slots, width = arrived.shape[1:]
    tile = w.shape[0] // tiles

    def row_copy(b):
        at = pl.ds(pl.multiple_of(b * peers, peers), peers)
        return pltpu.make_async_copy(rows_hbm.at[at], arrived.at[at], row_sems.at[b])

    def w_copy(n):
        at = pl.ds(pl.multiple_of(n * tile, tile), tile)
        return pltpu.make_async_copy(w_hbm.at[0, at, :], w.at[at, :], w_sems.at[n])

    halves = 2
    group = blocks // halves
    half = group * peers * slots

    def product(at, n):
        to = pl.ds(pl.multiple_of(n * tile, tile), tile)
        raw_ref[at, to] = lax.dot_general(
            rows[at, :], w[to, :], (((1,), (1,)), ((), ())), preferred_element_type=jnp.float32
        )

    for b in range(group):
        row_copy(b).start()
    w_copy(0).start()

    @pl.loop(0, halves)
    def _(h):
        @pl.loop(0, group)
        def _(g):
            b = h * group + g
            row_copy(b).wait()

            @pl.when(h == 0)
            def _():
                row_copy(group + g).start()

            at = pl.ds(pl.multiple_of(b * peers, peers), peers)
            to = pl.ds(pl.multiple_of(b * peers * slots, peers * slots), peers * slots)
            rows[to, :] = arrived[at].reshape(peers * slots, width)

        @pl.when(h == 0)
        def _():
            w_copy(0).wait()
            w_copy(1).start()

        product(pl.ds(pl.multiple_of(h * half, half), half), 0)

    @pl.loop(1, tiles)
    def _(n):
        w_copy(n).wait()

        @pl.when(n < tiles - 1)
        def _():
            w_copy(n + 1).start()

        product(slice(None), n)


def final_kernel(
    slots, raw_ref, back_ref, rank_ref, chosen_ref, hidden_hbm, logits_ref, hidden, out_sems
):
    blocks = out_sems.shape[0]
    block = raw_ref.shape[0] // blocks
    peers = block // slots
    lanes = back_ref.shape[1]

    def out_copy(b):
        at = pl.ds(b * block, block)
        return pltpu.make_async_copy(hidden.at[at, :], hidden_hbm.at[0, at, :], out_sems.at[b])

    spread = (iota((block, peers), 0) // slots == iota((block, peers), 1)).astype(jnp.bfloat16)
    slot = iota((block, lanes), 0) % slots
    mine = slot + slots == iota((block, lanes), 1)
    for b in range(blocks):
        sent = back_ref[b * peers : (b + 1) * peers, :].astype(jnp.bfloat16)
        weight = jnp.dot(spread, sent, preferred_element_type=jnp.float32)
        weight = jnp.sum(jnp.where(mine, weight, 0.0), 1, keepdims=True)
        at = slice(b * block, (b + 1) * block)
        hidden[at, :] = (weight * raw_ref[at, :]).astype(jnp.bfloat16)
        out_copy(b).start()
    rank = rank_ref[...]
    chosen = chosen_ref[...]
    total = jnp.sum(chosen, 1, keepdims=True)
    back = jnp.transpose(back_ref[...])
    per_route = jnp.zeros_like(chosen)
    for j in range(slots):
        per_route += jnp.where(rank == j + 1.0, back[j : j + 1, :], 0.0)
    mean_grad = jnp.sum(per_route * chosen, 1, keepdims=True) / total
    d_chosen = (route_scale / total) * (per_route - mean_grad)
    logits_ref[...] = jnp.where(rank > 0.0, d_chosen * chosen * (1.0 - chosen), 0.0)
    for b in range(blocks):
        out_copy(b).wait()


def params(size=24):
    return pltpu.CompilerParams(vmem_limit_bytes=size * MIB)


def in_hbm(array):
    return pltpu.with_memory_space_constraint(array, pltpu.HBM)


def shards(grad_out, logits, routes, w_down, saved_hidden):
    tokens, width = grad_out.shape
    experts = logits.shape[1]
    capacity, units = saved_hidden.shape[1:]
    slots = capacity // experts
    routes_t = routes.T
    near, far = pl.BlockSpec(memory_space=pltpu.VMEM), pl.BlockSpec(memory_space=pltpu.HBM)
    packed = (experts, slots, width)
    sent = pl.pallas_call(
        functools.partial(pack_kernel, slots),
        in_specs=[near, near],
        out_specs=far,
        out_shape=pltpu.HBM(packed, jnp.bfloat16),
        scratch_shapes=[pltpu.VMEM(packed, jnp.bfloat16), pltpu.SemaphoreType.DMA((7,))],
        compiler_params=params(),
        cost_estimate=pl.CostEstimate(
            flops=2 * capacity * width * tokens, bytes_accessed=2 * capacity * width, transcendentals=0
        ),
        name="pack",
    )(in_hbm(routes_t), in_hbm(grad_out))
    arrived = lax.all_to_all(sent, ("node", "expert"), split_axis=0, concat_axis=0, tiled=True)
    weights, rank, chosen = pl.pallas_call(
        functools.partial(weight_kernel, slots),
        out_shape=(
            jax.ShapeDtypeStruct((experts, experts), jnp.float32),
            jax.ShapeDtypeStruct((tokens, experts), jnp.float32),
            jax.ShapeDtypeStruct((tokens, experts), jnp.float32),
        ),
        compiler_params=params(),
        name="weights",
    )(routes_t, logits)
    span = 1024
    project = pl.pallas_call(
        project_kernel,
        grid=(width // span,),
        in_specs=[
            pl.BlockSpec((None, capacity, units), lambda i: (0, 0, 0)),
            pl.BlockSpec((None, units, span), lambda i: (0, 0, i)),
        ],
        out_specs=pl.BlockSpec((capacity, span), lambda i: (0, i)),
        out_shape=pltpu.HBM((capacity, width), jnp.bfloat16),
        compiler_params=params(),
        cost_estimate=pl.CostEstimate(
            flops=2 * capacity * units * width, bytes_accessed=2 * units * width, transcendentals=0
        ),
        name="project",
    )(saved_hidden, in_hbm(w_down))
    back = pl.pallas_call(
        return_kernel,
        in_specs=[far, far, near],
        out_specs=near,
        out_shape=jax.ShapeDtypeStruct((experts, experts), jnp.float32),
        scratch_shapes=[
            pltpu.VMEM(packed, jnp.bfloat16),
            pltpu.VMEM((capacity, width), jnp.bfloat16),
            pltpu.SemaphoreType.DMA((8,)),
            pltpu.SemaphoreType.DMA((8,)),
        ],
        compiler_params=params(),
        cost_estimate=pl.CostEstimate(
            flops=2 * capacity * width, bytes_accessed=4 * capacity * width, transcendentals=0
        ),
        name="return",
    )(in_hbm(arrived), in_hbm(project), weights)
    raw = pl.pallas_call(
        expert_kernel,
        in_specs=[far, far],
        out_shape=jax.ShapeDtypeStruct((capacity, units), jnp.float32),
        scratch_shapes=[
            pltpu.VMEM(packed, jnp.bfloat16),
            pltpu.VMEM((capacity, width), jnp.bfloat16),
            pltpu.VMEM((units, width), jnp.bfloat16),
            pltpu.SemaphoreType.DMA((8,)),
            pltpu.SemaphoreType.DMA((units // 256,)),
        ],
        compiler_params=params(48),
        cost_estimate=pl.CostEstimate(
            flops=2 * capacity * units * width,
            bytes_accessed=2 * (units + capacity) * width + 4 * capacity * units,
            transcendentals=0,
        ),
        name="expert",
    )(in_hbm(arrived), in_hbm(w_down))
    returned = lax.all_to_all(
        back.reshape(experts, 1, experts), ("node", "expert"), split_axis=0, concat_axis=0, tiled=True
    ).reshape(experts, experts)
    d_hidden, d_logits = pl.pallas_call(
        functools.partial(final_kernel, slots),
        in_specs=[near, near, near, near],
        out_specs=(far, near),
        out_shape=(
            jax.ShapeDtypeStruct((1, capacity, units), jnp.bfloat16),
            jax.ShapeDtypeStruct((tokens, experts), jnp.float32),
        ),
        scratch_shapes=[
            pltpu.VMEM((capacity, units), jnp.bfloat16),
            pltpu.SemaphoreType.DMA((4,)),
        ],
        compiler_params=params(),
        name="final",
    )(raw, returned, rank, chosen)
    return (d_hidden, d_logits)


def solution(mesh):
    return jax.shard_map(
        shards,
        mesh=mesh,
        in_specs=(
            P(("node", "expert"), None),
            P(("node", "expert"), None),
            P(("node", "expert"), None),
            P(("node", "expert"), None, None),
            P(("node", "expert"), None, None),
        ),
        out_specs=(P(("node", "expert"), None, None), P(("node", "expert"), None)),
        check_vma=False,
    )
```

```python
import functools

import jax
import jax.numpy as jnp
from jax import lax
from jax.experimental import pallas as pl
from jax.experimental.pallas import tpu as pltpu
from jax.sharding import PartitionSpec as P

route_scale = 2.5
MIB = 1 << 20


def iota(shape, dim):
    return lax.broadcasted_iota(jnp.int32, shape, dim)


def slot_ranks(routes_t, experts):
    most, tokens = routes_t.shape
    ids = iota((experts, tokens), 0)
    picked = jnp.zeros((experts, tokens), jnp.float32)
    for k in range(most):
        picked += (routes_t[k : k + 1, :] == ids).astype(jnp.float32)
    before = (iota((tokens, tokens), 0) < iota((tokens, tokens), 1)).astype(jnp.bfloat16)
    earlier = jnp.dot(picked.astype(jnp.bfloat16), before, preferred_element_type=jnp.float32)
    return picked * (earlier + 1.0)


def pack_kernel(slots, routes_ref, grad_ref, out_hbm, out, sems):
    tokens, width = grad_ref.shape
    experts = out.shape[0]
    rows = experts * slots
    rank = slot_ranks(routes_ref[...], experts)
    rank = jnp.broadcast_to(rank[:, None, :], (experts, slots, tokens)).reshape(rows, tokens)
    slot = (iota((rows, tokens), 0) % slots + 1).astype(jnp.float32)
    take = jnp.where(rank == slot, 1.0, 0.0).astype(jnp.bfloat16)
    parts = sems.shape[0]
    part = width // parts

    def copy(c):
        at = pl.ds(c * part, part)
        return pltpu.make_async_copy(out.at[:, :, at], out_hbm.at[:, :, at], sems.at[c])

    for c in range(parts):
        at = pl.ds(c * part, part)
        packed = jnp.dot(take, grad_ref[:, at], preferred_element_type=jnp.float32).astype(jnp.bfloat16)
        out[:, :, at] = packed.reshape(experts, slots, part)
        copy(c).start()
    for c in range(parts):
        copy(c).wait()


def weight_kernel(slots, routes_ref, logits_ref, out_ref, rank_ref, chosen_ref):
    tokens, experts = logits_ref.shape
    found = slot_ranks(routes_ref[...], experts).astype(jnp.bfloat16)
    unit = (iota((experts, experts), 0) == iota((experts, experts), 1)).astype(jnp.bfloat16)
    rank = lax.dot_general(found, unit, (((0,), (0,)), ((), ())), preferred_element_type=jnp.float32)
    rank_ref[...] = rank
    chosen = jnp.where(rank > 0.0, jax.nn.sigmoid(logits_ref[...]), 0.0)
    chosen_ref[...] = chosen
    total = jnp.sum(chosen, 1, keepdims=True)
    weights = (route_scale * chosen / total).astype(jnp.bfloat16).astype(jnp.float32)
    out = jnp.zeros((experts, experts), jnp.float32)
    lane = iota((tokens, experts), 1)
    for j in range(slots):
        mine = jnp.where(rank == j + 1.0, weights, 0.0).astype(jnp.bfloat16)
        to = (lane == slots + j).astype(jnp.bfloat16)
        out += lax.dot_general(mine, to, (((0,), (0,)), ((), ())), preferred_element_type=jnp.float32)
    out_ref[...] = out


def project_kernel(hidden_ref, w_ref, held_ref, out_ref):
    whole = jnp.dot(hidden_ref[...], w_ref[...], preferred_element_type=jnp.float32).astype(jnp.bfloat16)
    held = held_ref.shape[0]
    held_ref[...] = whole[:held]
    out_ref[...] = whole[held:]


def return_kernel(rows_hbm, kept_ref, project_hbm, weights_ref, back_ref, rows, project, row_sems, project_sems):
    blocks = row_sems.shape[0]
    slots, width = rows.shape[1:]
    peers = rows.shape[0] // blocks
    held = blocks - project_sems.shape[0]
    lanes = back_ref.shape[1]
    part, wide = 8, 1024

    def row_copy(b):
        at = pl.ds(pl.multiple_of(b * peers, peers), peers)
        return pltpu.make_async_copy(rows_hbm.at[at], rows.at[at], row_sems.at[b])

    def project_copy(b):
        at = pl.ds(pl.multiple_of(b * peers * slots, peers * slots), peers * slots)
        return pltpu.make_async_copy(project_hbm.at[at, :], project.at[at, :], project_sems.at[b])

    for b in range(blocks):
        row_copy(b).start()
        if b >= held:
            project_copy(b - held).start()

    def block(b, source, first):
        for start in range(0, peers, part):
            at = pl.ds(pl.multiple_of(b * peers + start, part), part)
            to = pl.ds(pl.multiple_of(((b - first) * peers + start) * slots, part * slots), part * slots)
            total = jnp.zeros((part * slots, lanes), jnp.float32)
            for begin in range(0, width, wide):
                columns = slice(begin, begin + wide)
                row = rows[at, :, columns].reshape(part * slots, wide).astype(jnp.float32)
                product = row * source[to, columns].astype(jnp.float32)
                for column in range(0, wide, lanes):
                    total += product[:, column : column + lanes]
            grads = jnp.sum(total, 1, keepdims=True)
            slot = iota((part * slots, lanes), 0) % slots
            spread = jnp.where(slot == iota((part * slots, lanes), 1), grads, 0.0)
            back_ref[at, :] = weights_ref[at, :] + jnp.sum(spread.reshape(part, slots, lanes), 1)

    @pl.loop(0, held)
    def _(b):
        row_copy(b).wait()
        block(b, kept_ref, 0)

    @pl.loop(held, blocks)
    def _(b):
        row_copy(b).wait()
        project_copy(b - held).wait()
        block(b, project, held)


def expert_kernel(rows_hbm, w_hbm, raw_ref, arrived, rows, w, row_sems, w_sems):
    blocks, tiles = row_sems.shape[0], w_sems.shape[0]
    peers = arrived.shape[0] // blocks
    slots, width = arrived.shape[1:]
    tile = w.shape[0] // tiles

    def row_copy(b):
        at = pl.ds(pl.multiple_of(b * peers, peers), peers)
        return pltpu.make_async_copy(rows_hbm.at[at], arrived.at[at], row_sems.at[b])

    def w_copy(n):
        at = pl.ds(pl.multiple_of(n * tile, tile), tile)
        return pltpu.make_async_copy(w_hbm.at[0, at, :], w.at[at, :], w_sems.at[n])

    halves = 2
    group = blocks // halves
    half = group * peers * slots

    def product(at, n):
        to = pl.ds(pl.multiple_of(n * tile, tile), tile)
        raw_ref[at, to] = lax.dot_general(
            rows[at, :], w[to, :], (((1,), (1,)), ((), ())), preferred_element_type=jnp.float32
        )

    for b in range(group):
        row_copy(b).start()
    w_copy(0).start()

    @pl.loop(0, halves)
    def _(h):
        @pl.loop(0, group)
        def _(g):
            b = h * group + g
            row_copy(b).wait()

            @pl.when(h == 0)
            def _():
                row_copy(group + g).start()

            at = pl.ds(pl.multiple_of(b * peers, peers), peers)
            to = pl.ds(pl.multiple_of(b * peers * slots, peers * slots), peers * slots)
            rows[to, :] = arrived[at].reshape(peers * slots, width)

        @pl.when(h == 0)
        def _():
            w_copy(0).wait()
            w_copy(1).start()

        product(pl.ds(pl.multiple_of(h * half, half), half), 0)

    @pl.loop(1, tiles)
    def _(n):
        w_copy(n).wait()

        @pl.when(n < tiles - 1)
        def _():
            w_copy(n + 1).start()

        product(slice(None), n)


def final_kernel(
    slots, raw_ref, back_ref, rank_ref, chosen_ref, hidden_hbm, logits_ref, hidden, out_sems
):
    blocks = out_sems.shape[0]
    block = raw_ref.shape[0] // blocks
    peers = block // slots
    lanes = back_ref.shape[1]

    def out_copy(b):
        at = pl.ds(b * block, block)
        return pltpu.make_async_copy(hidden.at[at, :], hidden_hbm.at[0, at, :], out_sems.at[b])

    spread = (iota((block, peers), 0) // slots == iota((block, peers), 1)).astype(jnp.bfloat16)
    slot = iota((block, lanes), 0) % slots
    mine = slot + slots == iota((block, lanes), 1)
    for b in range(blocks):
        sent = back_ref[b * peers : (b + 1) * peers, :].astype(jnp.bfloat16)
        weight = jnp.dot(spread, sent, preferred_element_type=jnp.float32)
        weight = jnp.sum(jnp.where(mine, weight, 0.0), 1, keepdims=True)
        at = slice(b * block, (b + 1) * block)
        hidden[at, :] = (weight * raw_ref[at, :]).astype(jnp.bfloat16)
        out_copy(b).start()
    rank = rank_ref[...]
    chosen = chosen_ref[...]
    total = jnp.sum(chosen, 1, keepdims=True)
    back = jnp.transpose(back_ref[...])
    per_route = jnp.zeros_like(chosen)
    for j in range(slots):
        per_route += jnp.where(rank == j + 1.0, back[j : j + 1, :], 0.0)
    mean_grad = jnp.sum(per_route * chosen, 1, keepdims=True) / total
    d_chosen = (route_scale / total) * (per_route - mean_grad)
    logits_ref[...] = jnp.where(rank > 0.0, d_chosen * chosen * (1.0 - chosen), 0.0)
    for b in range(blocks):
        out_copy(b).wait()


def params(size=24):
    return pltpu.CompilerParams(vmem_limit_bytes=size * MIB)


def in_hbm(array):
    return pltpu.with_memory_space_constraint(array, pltpu.HBM)


def shards(grad_out, logits, routes, w_down, saved_hidden):
    tokens, width = grad_out.shape
    experts = logits.shape[1]
    capacity, units = saved_hidden.shape[1:]
    slots = capacity // experts
    routes_t = routes.T
    near, far = pl.BlockSpec(memory_space=pltpu.VMEM), pl.BlockSpec(memory_space=pltpu.HBM)
    packed = (experts, slots, width)
    sent = pl.pallas_call(
        functools.partial(pack_kernel, slots),
        in_specs=[near, near],
        out_specs=far,
        out_shape=pltpu.HBM(packed, jnp.bfloat16),
        scratch_shapes=[pltpu.VMEM(packed, jnp.bfloat16), pltpu.SemaphoreType.DMA((7,))],
        compiler_params=params(),
        cost_estimate=pl.CostEstimate(
            flops=2 * capacity * width * tokens, bytes_accessed=2 * capacity * width, transcendentals=0
        ),
        name="pack",
    )(in_hbm(routes_t), in_hbm(grad_out))
    arrived = lax.all_to_all(sent, ("node", "expert"), split_axis=0, concat_axis=0, tiled=True)
    weights, rank, chosen = pl.pallas_call(
        functools.partial(weight_kernel, slots),
        out_shape=(
            jax.ShapeDtypeStruct((experts, experts), jnp.float32),
            jax.ShapeDtypeStruct((tokens, experts), jnp.float32),
            jax.ShapeDtypeStruct((tokens, experts), jnp.float32),
        ),
        compiler_params=params(),
        name="weights",
    )(routes_t, logits)
    span = 1024
    held = capacity * 3 // 8
    kept, project = pl.pallas_call(
        project_kernel,
        grid=(width // span,),
        in_specs=[
            pl.BlockSpec((None, capacity, units), lambda i: (0, 0, 0)),
            pl.BlockSpec((None, units, span), lambda i: (0, 0, i)),
        ],
        out_specs=(
            pl.BlockSpec((held, span), lambda i: (0, i)),
            pl.BlockSpec((capacity - held, span), lambda i: (0, i)),
        ),
        out_shape=(
            jax.ShapeDtypeStruct((held, width), jnp.bfloat16),
            pltpu.HBM((capacity - held, width), jnp.bfloat16),
        ),
        compiler_params=params(),
        cost_estimate=pl.CostEstimate(
            flops=2 * capacity * units * width, bytes_accessed=2 * units * width, transcendentals=0
        ),
        name="project",
    )(saved_hidden, in_hbm(w_down))
    back = pl.pallas_call(
        return_kernel,
        in_specs=[far, near, far, near],
        out_specs=near,
        out_shape=jax.ShapeDtypeStruct((experts, experts), jnp.float32),
        scratch_shapes=[
            pltpu.VMEM(packed, jnp.bfloat16),
            pltpu.VMEM((capacity - held, width), jnp.bfloat16),
            pltpu.SemaphoreType.DMA((8,)),
            pltpu.SemaphoreType.DMA((5,)),
        ],
        compiler_params=params(),
        cost_estimate=pl.CostEstimate(
            flops=2 * capacity * width, bytes_accessed=4 * capacity * width, transcendentals=0
        ),
        name="return",
    )(in_hbm(arrived), kept, in_hbm(project), weights)
    raw = pl.pallas_call(
        expert_kernel,
        in_specs=[far, far],
        out_shape=jax.ShapeDtypeStruct((capacity, units), jnp.float32),
        scratch_shapes=[
            pltpu.VMEM(packed, jnp.bfloat16),
            pltpu.VMEM((capacity, width), jnp.bfloat16),
            pltpu.VMEM((units, width), jnp.bfloat16),
            pltpu.SemaphoreType.DMA((8,)),
            pltpu.SemaphoreType.DMA((units // 256,)),
        ],
        compiler_params=params(48),
        cost_estimate=pl.CostEstimate(
            flops=2 * capacity * units * width,
            bytes_accessed=2 * (units + capacity) * width + 4 * capacity * units,
            transcendentals=0,
        ),
        name="expert",
    )(in_hbm(arrived), in_hbm(w_down))
    returned = lax.all_to_all(
        back.reshape(experts, 1, experts), ("node", "expert"), split_axis=0, concat_axis=0, tiled=True
    ).reshape(experts, experts)
    d_hidden, d_logits = pl.pallas_call(
        functools.partial(final_kernel, slots),
        in_specs=[near, near, near, near],
        out_specs=(far, near),
        out_shape=(
            jax.ShapeDtypeStruct((1, capacity, units), jnp.bfloat16),
            jax.ShapeDtypeStruct((tokens, experts), jnp.float32),
        ),
        scratch_shapes=[
            pltpu.VMEM((capacity, units), jnp.bfloat16),
            pltpu.SemaphoreType.DMA((4,)),
        ],
        compiler_params=params(),
        name="final",
    )(raw, returned, rank, chosen)
    return (d_hidden, d_logits)


def solution(mesh):
    return jax.shard_map(
        shards,
        mesh=mesh,
        in_specs=(
            P(("node", "expert"), None),
            P(("node", "expert"), None),
            P(("node", "expert"), None),
            P(("node", "expert"), None, None),
            P(("node", "expert"), None, None),
        ),
        out_specs=(P(("node", "expert"), None, None), P(("node", "expert"), None)),
        check_vma=False,
    )
```

```python
import functools

import jax
import jax.numpy as jnp
from jax import lax
from jax.experimental import pallas as pl
from jax.experimental.pallas import tpu as pltpu
from jax.sharding import PartitionSpec as P

route_scale = 2.5
MIB = 1 << 20


def iota(shape, dim):
    return lax.broadcasted_iota(jnp.int32, shape, dim)


def slot_ranks(routes_t, experts):
    most, tokens = routes_t.shape
    ids = iota((experts, tokens), 0)
    picked = jnp.zeros((experts, tokens), jnp.float32)
    for k in range(most):
        picked += (routes_t[k : k + 1, :] == ids).astype(jnp.float32)
    before = (iota((tokens, tokens), 0) < iota((tokens, tokens), 1)).astype(jnp.bfloat16)
    earlier = jnp.dot(picked.astype(jnp.bfloat16), before, preferred_element_type=jnp.float32)
    return picked * (earlier + 1.0)


def pack_kernel(slots, routes_ref, grad_ref, out_hbm, out, sems):
    tokens, width = grad_ref.shape
    experts = out.shape[0]
    rows = experts * slots
    rank = slot_ranks(routes_ref[...], experts)
    rank = jnp.broadcast_to(rank[:, None, :], (experts, slots, tokens)).reshape(rows, tokens)
    slot = (iota((rows, tokens), 0) % slots + 1).astype(jnp.float32)
    take = jnp.where(rank == slot, 1.0, 0.0).astype(jnp.bfloat16)
    parts = sems.shape[0]
    part = width // parts

    def copy(c):
        at = pl.ds(c * part, part)
        return pltpu.make_async_copy(out.at[:, :, at], out_hbm.at[:, :, at], sems.at[c])

    for c in range(parts):
        at = pl.ds(c * part, part)
        packed = jnp.dot(take, grad_ref[:, at], preferred_element_type=jnp.float32).astype(jnp.bfloat16)
        out[:, :, at] = packed.reshape(experts, slots, part)
        copy(c).start()
    for c in range(parts):
        copy(c).wait()


def weight_kernel(slots, routes_ref, logits_ref, out_ref, rank_ref, chosen_ref):
    tokens, experts = logits_ref.shape
    found = slot_ranks(routes_ref[...], experts).astype(jnp.bfloat16)
    unit = (iota((experts, experts), 0) == iota((experts, experts), 1)).astype(jnp.bfloat16)
    rank = lax.dot_general(found, unit, (((0,), (0,)), ((), ())), preferred_element_type=jnp.float32)
    rank_ref[...] = rank
    chosen = jnp.where(rank > 0.0, jax.nn.sigmoid(logits_ref[...]), 0.0)
    chosen_ref[...] = chosen
    total = jnp.sum(chosen, 1, keepdims=True)
    weights = (route_scale * chosen / total).astype(jnp.bfloat16).astype(jnp.float32)
    out = jnp.zeros((experts, experts), jnp.float32)
    lane = iota((tokens, experts), 1)
    for j in range(slots):
        mine = jnp.where(rank == j + 1.0, weights, 0.0).astype(jnp.bfloat16)
        to = (lane == slots + j).astype(jnp.bfloat16)
        out += lax.dot_general(mine, to, (((0,), (0,)), ((), ())), preferred_element_type=jnp.float32)
    out_ref[...] = out


def project_kernel(hidden_ref, w_ref, held_ref, out_ref):
    whole = jnp.dot(hidden_ref[...], w_ref[...], preferred_element_type=jnp.float32).astype(jnp.bfloat16)
    held = held_ref.shape[0]
    held_ref[...] = whole[:held]
    out_ref[...] = whole[held:]


def return_kernel(rows_hbm, kept_ref, project_hbm, weights_ref, back_ref, rows, project, row_sems, project_sems):
    blocks = row_sems.shape[0]
    slots, width = rows.shape[1:]
    peers = rows.shape[0] // blocks
    held = blocks - project_sems.shape[0]
    lanes = back_ref.shape[1]
    part, wide = 16, 512

    def row_copy(b):
        at = pl.ds(pl.multiple_of(b * peers, peers), peers)
        return pltpu.make_async_copy(rows_hbm.at[at], rows.at[at], row_sems.at[b])

    def project_copy(b):
        at = pl.ds(pl.multiple_of(b * peers * slots, peers * slots), peers * slots)
        return pltpu.make_async_copy(project_hbm.at[at, :], project.at[at, :], project_sems.at[b])

    for b in range(blocks):
        row_copy(b).start()
        if b >= held:
            project_copy(b - held).start()

    def block(b, source, first):
        for start in range(0, peers, part):
            at = pl.ds(pl.multiple_of(b * peers + start, part), part)
            to = pl.ds(pl.multiple_of(((b - first) * peers + start) * slots, part * slots), part * slots)
            total = jnp.zeros((part * slots, lanes), jnp.float32)
            for begin in range(0, width, wide):
                columns = slice(begin, begin + wide)
                row = rows[at, :, columns].reshape(part * slots, wide).astype(jnp.float32)
                product = row * source[to, columns].astype(jnp.float32)
                for column in range(0, wide, lanes):
                    total += product[:, column : column + lanes]
            grads = jnp.sum(total, 1, keepdims=True)
            slot = iota((part * slots, lanes), 0) % slots
            spread = jnp.where(slot == iota((part * slots, lanes), 1), grads, 0.0)
            back_ref[at, :] = weights_ref[at, :] + jnp.sum(spread.reshape(part, slots, lanes), 1)

    @pl.loop(0, held)
    def _(b):
        row_copy(b).wait()
        block(b, kept_ref, 0)

    @pl.loop(held, blocks)
    def _(b):
        row_copy(b).wait()
        project_copy(b - held).wait()
        block(b, project, held)


def expert_kernel(rows_hbm, w_hbm, raw_ref, arrived, rows, w, row_sems, w_sems):
    blocks, tiles = row_sems.shape[0], w_sems.shape[0]
    peers = arrived.shape[0] // blocks
    slots, width = arrived.shape[1:]
    tile = w.shape[0] // tiles

    def row_copy(b):
        at = pl.ds(pl.multiple_of(b * peers, peers), peers)
        return pltpu.make_async_copy(rows_hbm.at[at], arrived.at[at], row_sems.at[b])

    def w_copy(n):
        at = pl.ds(pl.multiple_of(n * tile, tile), tile)
        return pltpu.make_async_copy(w_hbm.at[0, at, :], w.at[at, :], w_sems.at[n])

    halves = 2
    group = blocks // halves
    half = group * peers * slots

    def product(at, n):
        to = pl.ds(pl.multiple_of(n * tile, tile), tile)
        raw_ref[at, to] = lax.dot_general(
            rows[at, :], w[to, :], (((1,), (1,)), ((), ())), preferred_element_type=jnp.float32
        )

    for b in range(group):
        row_copy(b).start()
    w_copy(0).start()

    @pl.loop(0, halves)
    def _(h):
        @pl.loop(0, group)
        def _(g):
            b = h * group + g
            row_copy(b).wait()

            @pl.when(h == 0)
            def _():
                row_copy(group + g).start()

            at = pl.ds(pl.multiple_of(b * peers, peers), peers)
            to = pl.ds(pl.multiple_of(b * peers * slots, peers * slots), peers * slots)
            rows[to, :] = arrived[at].reshape(peers * slots, width)

        @pl.when(h == 0)
        def _():
            w_copy(0).wait()
            w_copy(1).start()

        product(pl.ds(pl.multiple_of(h * half, half), half), 0)

    @pl.loop(1, tiles)
    def _(n):
        w_copy(n).wait()

        @pl.when(n < tiles - 1)
        def _():
            w_copy(n + 1).start()

        product(slice(None), n)


def final_kernel(
    slots, raw_ref, back_ref, rank_ref, chosen_ref, hidden_hbm, logits_ref, hidden, out_sems
):
    blocks = out_sems.shape[0]
    block = raw_ref.shape[0] // blocks
    peers = block // slots
    lanes = back_ref.shape[1]

    def out_copy(b):
        at = pl.ds(b * block, block)
        return pltpu.make_async_copy(hidden.at[at, :], hidden_hbm.at[0, at, :], out_sems.at[b])

    spread = (iota((block, peers), 0) // slots == iota((block, peers), 1)).astype(jnp.bfloat16)
    slot = iota((block, lanes), 0) % slots
    mine = slot + slots == iota((block, lanes), 1)
    for b in range(blocks):
        sent = back_ref[b * peers : (b + 1) * peers, :].astype(jnp.bfloat16)
        weight = jnp.dot(spread, sent, preferred_element_type=jnp.float32)
        weight = jnp.sum(jnp.where(mine, weight, 0.0), 1, keepdims=True)
        at = slice(b * block, (b + 1) * block)
        hidden[at, :] = (weight * raw_ref[at, :]).astype(jnp.bfloat16)
        out_copy(b).start()
    rank = rank_ref[...]
    chosen = chosen_ref[...]
    total = jnp.sum(chosen, 1, keepdims=True)
    back = jnp.transpose(back_ref[...])
    per_route = jnp.zeros_like(chosen)
    for j in range(slots):
        per_route += jnp.where(rank == j + 1.0, back[j : j + 1, :], 0.0)
    mean_grad = jnp.sum(per_route * chosen, 1, keepdims=True) / total
    d_chosen = (route_scale / total) * (per_route - mean_grad)
    logits_ref[...] = jnp.where(rank > 0.0, d_chosen * chosen * (1.0 - chosen), 0.0)
    for b in range(blocks):
        out_copy(b).wait()


def params(size=24):
    return pltpu.CompilerParams(vmem_limit_bytes=size * MIB)


def in_hbm(array):
    return pltpu.with_memory_space_constraint(array, pltpu.HBM)


def shards(grad_out, logits, routes, w_down, saved_hidden):
    tokens, width = grad_out.shape
    experts = logits.shape[1]
    capacity, units = saved_hidden.shape[1:]
    slots = capacity // experts
    routes_t = routes.T
    near, far = pl.BlockSpec(memory_space=pltpu.VMEM), pl.BlockSpec(memory_space=pltpu.HBM)
    packed = (experts, slots, width)
    sent = pl.pallas_call(
        functools.partial(pack_kernel, slots),
        in_specs=[near, near],
        out_specs=far,
        out_shape=pltpu.HBM(packed, jnp.bfloat16),
        scratch_shapes=[pltpu.VMEM(packed, jnp.bfloat16), pltpu.SemaphoreType.DMA((7,))],
        compiler_params=params(),
        cost_estimate=pl.CostEstimate(
            flops=2 * capacity * width * tokens, bytes_accessed=2 * capacity * width, transcendentals=0
        ),
        name="pack",
    )(in_hbm(routes_t), in_hbm(grad_out))
    arrived = lax.all_to_all(sent, ("node", "expert"), split_axis=0, concat_axis=0, tiled=True)
    weights, rank, chosen = pl.pallas_call(
        functools.partial(weight_kernel, slots),
        out_shape=(
            jax.ShapeDtypeStruct((experts, experts), jnp.float32),
            jax.ShapeDtypeStruct((tokens, experts), jnp.float32),
            jax.ShapeDtypeStruct((tokens, experts), jnp.float32),
        ),
        compiler_params=params(),
        name="weights",
    )(routes_t, logits)
    span = 1024
    held = capacity * 3 // 8
    kept, project = pl.pallas_call(
        project_kernel,
        grid=(width // span,),
        in_specs=[
            pl.BlockSpec((None, capacity, units), lambda i: (0, 0, 0)),
            pl.BlockSpec((None, units, span), lambda i: (0, 0, i)),
        ],
        out_specs=(
            pl.BlockSpec((held, span), lambda i: (0, i)),
            pl.BlockSpec((capacity - held, span), lambda i: (0, i)),
        ),
        out_shape=(
            jax.ShapeDtypeStruct((held, width), jnp.bfloat16),
            pltpu.HBM((capacity - held, width), jnp.bfloat16),
        ),
        compiler_params=params(),
        cost_estimate=pl.CostEstimate(
            flops=2 * capacity * units * width, bytes_accessed=2 * units * width, transcendentals=0
        ),
        name="project",
    )(saved_hidden, in_hbm(w_down))
    back = pl.pallas_call(
        return_kernel,
        in_specs=[far, near, far, near],
        out_specs=near,
        out_shape=jax.ShapeDtypeStruct((experts, experts), jnp.float32),
        scratch_shapes=[
            pltpu.VMEM(packed, jnp.bfloat16),
            pltpu.VMEM((capacity - held, width), jnp.bfloat16),
            pltpu.SemaphoreType.DMA((8,)),
            pltpu.SemaphoreType.DMA((5,)),
        ],
        compiler_params=params(),
        cost_estimate=pl.CostEstimate(
            flops=2 * capacity * width, bytes_accessed=4 * capacity * width, transcendentals=0
        ),
        name="return",
    )(in_hbm(arrived), kept, in_hbm(project), weights)
    raw = pl.pallas_call(
        expert_kernel,
        in_specs=[far, far],
        out_shape=jax.ShapeDtypeStruct((capacity, units), jnp.float32),
        scratch_shapes=[
            pltpu.VMEM(packed, jnp.bfloat16),
            pltpu.VMEM((capacity, width), jnp.bfloat16),
            pltpu.VMEM((units, width), jnp.bfloat16),
            pltpu.SemaphoreType.DMA((8,)),
            pltpu.SemaphoreType.DMA((units // 256,)),
        ],
        compiler_params=params(48),
        cost_estimate=pl.CostEstimate(
            flops=2 * capacity * units * width,
            bytes_accessed=2 * (units + capacity) * width + 4 * capacity * units,
            transcendentals=0,
        ),
        name="expert",
    )(in_hbm(arrived), in_hbm(w_down))
    returned = lax.all_to_all(
        back.reshape(experts, 1, experts), ("node", "expert"), split_axis=0, concat_axis=0, tiled=True
    ).reshape(experts, experts)
    d_hidden, d_logits = pl.pallas_call(
        functools.partial(final_kernel, slots),
        in_specs=[near, near, near, near],
        out_specs=(far, near),
        out_shape=(
            jax.ShapeDtypeStruct((1, capacity, units), jnp.bfloat16),
            jax.ShapeDtypeStruct((tokens, experts), jnp.float32),
        ),
        scratch_shapes=[
            pltpu.VMEM((capacity, units), jnp.bfloat16),
            pltpu.SemaphoreType.DMA((8,)),
        ],
        compiler_params=params(),
        name="final",
    )(raw, returned, rank, chosen)
    return (d_hidden, d_logits)


def solution(mesh):
    return jax.shard_map(
        shards,
        mesh=mesh,
        in_specs=(
            P(("node", "expert"), None),
            P(("node", "expert"), None),
            P(("node", "expert"), None),
            P(("node", "expert"), None, None),
            P(("node", "expert"), None, None),
        ),
        out_specs=(P(("node", "expert"), None, None), P(("node", "expert"), None)),
        check_vma=False,
    )
```
